256 devices in a mesh: row: 32 (over z, x_hi, core), col: 8 (over x_lo, y).
Axes of the slice: x: 4 (x_hi: 2, x_lo: 2; x = x_hi * 2 + x_lo), y: 4, z: 8, core: 2. Of those that a mesh axis runs over, the one named last changes fastest.
Arguments:
- features: bfloat16 [65536, 256], P(('row', 'col')), may hold values from -6 to 6
- w_out: bfloat16 [256, 256], replicated, may hold values from -0.375 to 0.375
- w_in: bfloat16 [256, 256], replicated, may hold values from -0.375 to 0.375
- tile_slot: int32 [32, 8, 16], P('row', 'col'), may hold values from 0 to 255, as said below
- tile_count: int32 [32, 8], P('row', 'col'), may hold values from 2 to 16, as said below
- tile_values: bfloat16 [32, 8, 16, 256, 256], P('row', 'col'), may hold values from -0.125 to 0.125
- cotangent: bfloat16 [65536, 256], P(('row', 'col')), may hold values from -6 to 6
Outputs:
- activated: bfloat16 [65536, 256], P(('row', 'col'))
- grad_features: bfloat16 [65536, 256], P(('row', 'col'))
- grad_w_out: float32 [256, 256], replicated
- grad_w_in: float32 [256, 256], replicated
The draws below stay inside these ranges and needn't reach their ends.
Inputs may be any that keep to these rules, and one draw needn't show every extreme that they name: `tile_slot`: within one device's list the 16 slots are distinct; slot s is tile row s // 32 and tile column s % 32 of that device's block; only the first tile_count entries are used. `tile_count`: in every draw some device has exactly 16 tiles.
All inputs are finite; a program needn't handle non-finite values.
Results may differ from the reference program's by a relative error of at most 0.0049.
Values may be sent and summed in bfloat16 or wider, within the bound.
No kernel may reach another device: no remote copies, remote signals or barrier semaphores. Data moves between devices by JAX's collectives and lax.ppermute only.
A program may use at most 128 MiB of HBM per device.

```python
import jax
import jax.numpy as jnp
from jax import lax

F = 256
TILE = 256
NODE_DEV = 256
ROW_SPAN = 2048
COL_SPAN = 8192
ROW_TILES = 8
COL_TILES = 32
TMAX = 16
NODES = 65536
N_ROW = 32
N_COL = 8


def draw_tile_slot(key, part):
    key = jax.random.fold_in(key, 11)
    device_keys = jax.random.split(key, N_ROW * N_COL)
    chosen = jax.vmap(lambda one_key: jax.random.permutation(one_key, ROW_TILES * COL_TILES)[:TMAX])(device_keys)
    return chosen.reshape(N_ROW, N_COL, TMAX).astype(jnp.int32)


def draw_tile_count(key, part):
    key = jax.random.fold_in(key, 23)
    key_light, key_heavy, key_pick, key_full = jax.random.split(key, 4)
    grid_shape = (N_ROW, N_COL)
    light_count = jax.random.randint(key_light, grid_shape, TMAX // 8, TMAX // 2 + 1)
    heavy_count = jax.random.randint(key_heavy, grid_shape, TMAX // 2, TMAX + 1)
    chooser = jax.random.randint(key_pick, grid_shape, 0, 8)
    counts = jnp.where(chooser == 0, heavy_count, light_count).reshape(-1)
    full_device = jax.random.randint(key_full, (), 0, N_ROW * N_COL)
    flat_counts = jnp.where(jnp.arange(N_ROW * N_COL) == full_device, TMAX, counts)
    return flat_counts.reshape(grid_shape).astype(jnp.int32)


def shard_levels(own_key, extent, cuts, smallest, largest):
    level = 1.0
    for position, parts in cuts:
        draws = jax.random.uniform(jax.random.fold_in(jax.random.fold_in(own_key, 6), position), (parts,), jnp.float32, smallest / len(cuts), largest / len(cuts))
        level = level * jnp.repeat(jnp.exp(draws), extent[position] // parts).reshape((-1,) + (1,) * (len(extent) - 1 - position))
    return level


def centred(key, shape, deviation, bound, pieces=(), dtype=jnp.bfloat16):
    factor_of = shard_levels(key, shape, pieces, -0.22, 0.18) if pieces else 1.0
    result = jax.random.normal(key, shape, jnp.float32) * deviation * factor_of
    return jnp.minimum(jnp.maximum(result, -bound), bound).astype(dtype)


def setup_inputs(seed: int = 0) -> dict:
    key_list = jax.random.split(jax.random.key(seed), 8)
    features = centred(key_list[0], (NODES, F), 1.0, 6.0, ((0, 256),))
    w_out = centred(key_list[1], (F, F), F ** -0.5, 0.375)
    w_in = centred(key_list[2], (F, F), F ** -0.5, 0.375)
    tile_slot = draw_tile_slot(jax.random.fold_in(key_list[7], 71), 0)
    tile_count = draw_tile_count(jax.random.fold_in(key_list[7], 71), 0)
    tile_values = centred(key_list[5], (N_ROW, N_COL, TMAX, TILE, TILE), (TMAX * TILE // 2) ** -0.5, 0.125, ((0, 32), (1, 8)))
    cotangent = centred(key_list[6], (NODES, F), 1.0, 6.0, ((0, 256),))
    return dict(features=features, w_out=w_out, w_in=w_in, tile_slot=tile_slot, tile_count=tile_count, tile_values=tile_values, cotangent=cotangent)


def block_terms(tile_slots, live_count, values, column_side, row_side):
    tile_row = tile_slots // COL_TILES
    tile_col = tile_slots % COL_TILES
    live_mask = (lax.iota(jnp.int32, TMAX) < live_count).astype(jnp.float32)
    col_blocks = column_side.reshape(COL_TILES, TILE, F)[tile_col].astype(jnp.float32)
    row_blocks = row_side.reshape(ROW_TILES, TILE, F)[tile_row].astype(jnp.float32)
    values_f32 = values.astype(jnp.float32)
    forward = jnp.einsum("kij,kjf->kif", values_f32, col_blocks, precision=lax.Precision.HIGHEST)
    transposed = jnp.einsum("kij,kif->kjf", values_f32, row_blocks, precision=lax.Precision.HIGHEST)
    pick_rows = (tile_row[:, None] == lax.iota(jnp.int32, ROW_TILES)[None, :]).astype(jnp.float32) * live_mask[:, None]
    pick_cols = (tile_col[:, None] == lax.iota(jnp.int32, COL_TILES)[None, :]).astype(jnp.float32) * live_mask[:, None]
    forward_sum = jnp.einsum("kt,kif->tif", pick_rows, forward, precision=lax.Precision.HIGHEST)
    transposed_sum = jnp.einsum("kt,kif->tif", pick_cols, transposed, precision=lax.Precision.HIGHEST)
    return forward_sum.reshape(ROW_SPAN, F), transposed_sum.reshape(COL_SPAN, F)


def propagate(source, tile_slot, tile_count, tile_values):
    blocks = source.reshape(N_ROW, N_COL, NODE_DEV, F)

    def one_device(device, totals):
        out_total, in_total = totals
        row_index = (device // N_COL).astype(jnp.int32)
        col_index = (device % N_COL).astype(jnp.int32)
        row_side = lax.dynamic_index_in_dim(blocks, row_index, 0, False).reshape(ROW_SPAN, F)
        column_side = lax.dynamic_index_in_dim(blocks, col_index, 1, False).reshape(COL_SPAN, F)
        slot_row = lax.dynamic_index_in_dim(tile_slot, row_index, 0, False)
        tile_slots = lax.dynamic_index_in_dim(slot_row, col_index, 0, False)
        count_row = lax.dynamic_index_in_dim(tile_count, row_index, 0, False)
        live_count = lax.dynamic_index_in_dim(count_row, col_index, 0, False)
        value_row = lax.dynamic_index_in_dim(tile_values, row_index, 0, False)
        values = lax.dynamic_index_in_dim(value_row, col_index, 0, False)
        forward_sum, transposed_sum = block_terms(tile_slots, live_count, values, column_side, row_side)
        out_total = out_total.at[row_index].add(forward_sum)
        in_total = in_total.at[:, col_index].add(transposed_sum.reshape(N_ROW, NODE_DEV, F))
        return out_total, in_total

    start_totals = (jnp.zeros((N_ROW, ROW_SPAN, F), jnp.float32), jnp.zeros((N_ROW, N_COL, NODE_DEV, F), jnp.float32))
    out_total, in_total = lax.fori_loop(0, N_ROW * N_COL, one_device, start_totals)
    return out_total.reshape(NODES, F), in_total.reshape(NODES, F)


def reference(features, w_out, w_in, tile_slot, tile_count, tile_values, cotangent):
    out_sum, in_sum = propagate(features, tile_slot, tile_count, tile_values)
    weight_out = w_out.astype(jnp.float32)
    weight_in = w_in.astype(jnp.float32)
    before = jnp.dot(out_sum, weight_out, precision=lax.Precision.HIGHEST) + jnp.dot(in_sum, weight_in, precision=lax.Precision.HIGHEST)
    sigmoid_of = jax.nn.sigmoid(before)
    activated = (before * sigmoid_of).astype(jnp.bfloat16)
    grad_before = (cotangent.astype(jnp.float32) * sigmoid_of * (1.0 + before * (1.0 - sigmoid_of))).astype(jnp.bfloat16)
    grad_f32 = grad_before.astype(jnp.float32)
    grad_w_out = jnp.einsum("nf,ng->fg", out_sum, grad_f32, precision=lax.Precision.HIGHEST)
    grad_w_in = jnp.einsum("nf,ng->fg", in_sum, grad_f32, precision=lax.Precision.HIGHEST)
    back_forward, back_transposed = propagate(grad_before, tile_slot, tile_count, tile_values)
    grad_features = jnp.einsum("ng,fg->nf", back_transposed, weight_out, precision=lax.Precision.HIGHEST) + jnp.einsum("ng,fg->nf", back_forward, weight_in, precision=lax.Precision.HIGHEST)
    return activated, grad_features.astype(jnp.bfloat16), grad_w_out, grad_w_in
```

```python
import functools

import jax
import jax.numpy as jnp
from jax import lax
from jax.experimental import pallas as pl
from jax.experimental.pallas import tpu as pltpu
from jax.sharding import PartitionSpec as P

TILE = 256
HALF = TILE // 2
LISTED = 16
F32 = jnp.float32
BF16 = jnp.bfloat16

ROWS = 32
COLS = 8


def row_move(dz, flip_hi, flip_core):
    pairs = []
    for r in range(ROWS):
        z, hi, core = r // 4, (r // 2) % 2, r % 2
        pairs.append((r, (((z + dz) % 8) * 2 + (hi ^ flip_hi)) * 2 + (core ^ flip_core)))
    return pairs


def col_move(dy, flip_lo):
    return [(c, (c // 4 ^ flip_lo) * 4 + (c % 4 + dy) % 4) for c in range(COLS)]


def z_up(x):
    return lax.ppermute(x, "row", row_move(1, 0, 0))


def z_down(x):
    return lax.ppermute(x, "row", row_move(-1, 0, 0))


def swap_hi(x):
    return lax.ppermute(x, "row", row_move(0, 1, 0))


def swap_core(x):
    return lax.ppermute(x, "row", row_move(0, 0, 1))


def y_up(x):
    return lax.ppermute(x, "col", col_move(1, 0))


def y_down(x):
    return lax.ppermute(x, "col", col_move(-1, 0))


def swap_lo(x):
    return lax.ppermute(x, "col", col_move(0, 1))


COUNTS = 2 * LISTED
PLACE = COUNTS + 2


def for_each_tile(meta, body):
    z, hi, core, lo, y = (meta[PLACE + i] for i in range(5))
    for which in range(2):

        def step(k, carry):
            slot = meta[which * LISTED + k]
            tile_row = slot // ROWS
            tile_col = slot % ROWS

            @pl.when((tile_col & 1) == core)
            def _():
                row_at = which * 8 + ((tile_row >> 2) ^ lo) * 4 + (((tile_row & 3) - y) & 3)
                col_at = (((tile_col >> 1) & 1) ^ hi) * 8 + (((tile_col >> 2) - z) & 7)
                body(which, k, row_at, col_at)

            return carry

        lax.fori_loop(0, meta[COUNTS + which], step, 0)


def transposed_kernel(meta, own_tiles, other_tiles, *refs):
    sources, out, side = refs[:16], refs[16], refs[17]
    for i in range(16):
        side[i] = sources[i][...]
    out[...] = jnp.zeros_like(out)

    def body(which, k, row_at, col_at):
        tiles = (own_tiles, other_tiles)[which]
        out[col_at] += lax.dot_general(
            tiles[k], side[row_at], (((0,), (0,)), ((), ())), preferred_element_type=F32
        )

    for_each_tile(meta, body)


def forward_kernel(meta, own_tiles, other_tiles, *refs):
    sources, out, side = refs[:18], refs[18], refs[19]
    for family in range(2):
        part = sources[family * 9 : family * 9 + 9]
        for i, d in enumerate((0, 1, 2, 3)):
            side[family * 8 + d] = part[i][...]
        for i, d in enumerate((5, 6, 7)):
            side[family * 8 + d] = part[4 + i][...]
        side[family * 8 + 4, :HALF] = part[7][...]
        side[family * 8 + 4, HALF:] = part[8][...]
    out[...] = jnp.zeros_like(out)

    def body(which, k, row_at, col_at):
        tiles = (own_tiles, other_tiles)[which]
        out[row_at] += jnp.dot(tiles[k], side[col_at], preferred_element_type=F32)

    for_each_tile(meta, body)


def tile_call(kernel, meta, own_tiles, other_tiles, sources):
    vmem = pl.BlockSpec(memory_space=pltpu.VMEM)
    return pl.pallas_call(
        kernel,
        out_shape=jax.ShapeDtypeStruct((16, TILE, TILE), F32),
        in_specs=[pl.BlockSpec(memory_space=pltpu.SMEM)] + [vmem] * (2 + len(sources)),
        out_specs=vmem,
        scratch_shapes=[pltpu.VMEM((16, TILE, TILE), BF16)],
        compiler_params=pltpu.CompilerParams(vmem_limit_bytes=40 * 2**20),
        cost_estimate=pl.CostEstimate(
            flops=16 * 2 * TILE**3, bytes_accessed=10 * 2**20, transcendentals=0
        ),
    )(meta, own_tiles, other_tiles, *sources)


def split(x):
    high = x.astype(BF16)
    return high, (x - high.astype(F32)).astype(BF16)


def dot2(x, y, dims):
    high, low = split(x)
    return lax.dot_general(high, y, (dims, ((), ())), preferred_element_type=F32) + lax.dot_general(
        low, y, (dims, ((), ())), preferred_element_type=F32
    )


def total_of(refs):
    total = refs[0][...].astype(F32)
    for ref in refs[1:]:
        total = total + ref[...].astype(F32)
    return total


def middle_kernel(n_out, *refs):
    out_parts, in_parts = refs[:n_out], refs[n_out : 2 * n_out]
    w_out, w_in, cotangent, activated, grad_before, local_out, local_in = refs[2 * n_out :]
    out_sum = total_of(out_parts)
    in_sum = total_of(in_parts)
    before = dot2(out_sum, w_out[...], ((1,), (0,))) + dot2(in_sum, w_in[...], ((1,), (0,)))
    gate = jax.nn.sigmoid(before)
    activated[...] = (before * gate).astype(BF16)
    grad = (cotangent[...].astype(F32) * gate * (1.0 + before * (1.0 - gate))).astype(BF16)
    grad_before[...] = grad
    local_out[...] = dot2(out_sum, grad, ((0,), (0,)))
    local_in[...] = dot2(in_sum, grad, ((0,), (0,)))


def end_kernel(n_out, *refs):
    forward_parts, transposed_parts = refs[:n_out], refs[n_out : 2 * n_out]
    w_out, w_in, grad_features = refs[2 * n_out :]
    back_forward = total_of(forward_parts)
    back_transposed = total_of(transposed_parts)
    grad_features[...] = (
        dot2(back_transposed, w_out[...], ((1,), (1,)))
        + dot2(back_forward, w_in[...], ((1,), (1,)))
    ).astype(BF16)


def dense_call(kernel, out_shape, operands):
    vmem = pl.BlockSpec(memory_space=pltpu.VMEM)
    return pl.pallas_call(
        kernel,
        out_shape=out_shape,
        in_specs=[vmem] * len(operands),
        out_specs=jax.tree.map(lambda _: vmem, out_shape),
        compiler_params=pltpu.CompilerParams(vmem_limit_bytes=32 * 2**20),
        cost_estimate=pl.CostEstimate(
            flops=8 * 2 * TILE**3, bytes_accessed=2 * 2**20, transcendentals=TILE * TILE
        ),
    )(*operands)


def gather_z(block):
    below, above = [], []
    up, down = block, block
    for _ in range(3):
        up, down = z_up(up), z_down(down)
        below.append(up)
        above.append(down)
    top, bottom = z_up(up[:HALF]), z_down(down[HALF:])
    return [block] + above + below[::-1] + [top, bottom]


def scatter_z(parts):
    up = z_up(parts[4, :HALF].astype(BF16))
    down = z_down(parts[4, HALF:].astype(BF16))
    up = jnp.concatenate([parts[3, :HALF] + up.astype(F32), parts[3, HALF:]])
    down = jnp.concatenate([parts[5, :HALF], parts[5, HALF:] + down.astype(F32)])
    up, down = z_up(up.astype(BF16)), z_down(down.astype(BF16))
    for d in (2, 1):
        up = z_up((parts[d] + up.astype(F32)).astype(BF16))
        down = z_down((parts[8 - d] + down.astype(F32)).astype(BF16))
    return parts[0], up, down


def gather_y(block, opposite_up):
    below, above = y_up(block), y_down(block)
    opposite = y_up(below) if opposite_up else y_down(above)
    return [block, above, opposite, below]


def scatter_y(parts, opposite_up):
    if opposite_up:
        up = parts[1] + y_up(parts[2].astype(BF16)).astype(F32)
        down = parts[3]
    else:
        up = parts[1]
        down = parts[3] + y_down(parts[2].astype(BF16)).astype(F32)
    return parts[0], y_up(up.astype(BF16)), y_down(down.astype(BF16))


def f32_sum(terms):
    total = terms[0].astype(F32)
    for term in terms[1:]:
        total = total + term.astype(F32)
    return total


def propagate(source, meta, own_tiles, other_tiles):
    other_lo = swap_lo(source)
    other_hi = swap_hi(source)
    row_blocks = gather_y(source, True) + gather_y(other_lo, False)
    row_blocks = row_blocks + [swap_core(block) for block in row_blocks]
    col_blocks = gather_z(source) + gather_z(other_hi)

    transposed = tile_call(transposed_kernel, meta, own_tiles, other_tiles, row_blocks)
    far = f32_sum(scatter_z(transposed[8:]))
    in_terms = scatter_z(transposed[:8]) + (swap_hi(far.astype(BF16)),)

    forward = tile_call(forward_kernel, meta, own_tiles, other_tiles, col_blocks)
    rows = forward[:8] + swap_core(forward[8:])
    far = f32_sum(scatter_y(rows[4:], False))
    out_terms = scatter_y(rows[:4], True) + (swap_lo(far.astype(BF16)),)
    return list(out_terms), list(in_terms)


def reduce_direct(x, axis, moves):
    total = x[0]
    for j in range(1, x.shape[0]):
        total = total + lax.ppermute(x[j], axis, moves(j))
    return total


def gather_direct(x, axis, moves, n):
    return [x] + [lax.ppermute(x, axis, moves(j)) for j in range(1, n)]


def roll_pieces(pieces, at):
    stacked = jnp.stack(pieces[::-1])
    return jnp.roll(stacked, at + 1, axis=0)


def sum_everywhere(local_out, local_in):
    row, col = lax.axis_index("row"), lax.axis_index("col")
    z, hi, core = row // 4, (row // 2) % 2, row % 2
    lo, y = col // 4, col % 4

    def by_core(x):
        return lax.dynamic_index_in_dim(x, core, 0, False)

    both = jnp.stack([local_out, local_in])
    keep = by_core(both)
    give = by_core(both[::-1])
    mine = keep + swap_core(give)

    def y_moves(j):
        return col_move(j, 0)

    def z_moves(j):
        return row_move(j, 0, 0)

    by_y = jnp.roll(mine.reshape(4, 64, TILE), -y, axis=0)
    mine = reduce_direct(by_y, "col", y_moves)
    by_z = jnp.roll(mine.reshape(8, 8, TILE), -z, axis=0)
    mine = reduce_direct(by_z, "row", z_moves)
    mine = mine + swap_lo(mine)
    mine = mine + swap_hi(mine)

    mine = roll_pieces(gather_direct(mine, "row", z_moves, 8), z).reshape(64, TILE)
    mine = roll_pieces(gather_direct(mine, "col", y_moves, 4), y).reshape(TILE, TILE)
    theirs = swap_core(mine)
    first = core == 0
    return jnp.where(first, mine, theirs), jnp.where(first, theirs, mine)


def local(features, w_out, w_in, tile_slot, tile_count, tile_values, cotangent):
    own_tiles = tile_values[0, 0]
    row, col = lax.axis_index("row"), lax.axis_index("col")
    own_list = jnp.concatenate([tile_slot[0, 0], tile_count[0]])
    other_list = swap_core(own_list)
    other_tiles = swap_core(own_tiles)
    place = jnp.stack([row // 4, (row // 2) % 2, row % 2, col // 4, col % 4]).astype(jnp.int32)
    meta = jnp.concatenate(
        [own_list[:LISTED], other_list[:LISTED], own_list[LISTED:], other_list[LISTED:], place]
    )

    out_terms, in_terms = propagate(features, meta, own_tiles, other_tiles)
    block = (TILE, TILE)
    activated, grad_before, local_out, local_in = dense_call(
        functools.partial(middle_kernel, len(out_terms)),
        (
            jax.ShapeDtypeStruct(block, BF16),
            jax.ShapeDtypeStruct(block, BF16),
            jax.ShapeDtypeStruct(block, F32),
            jax.ShapeDtypeStruct(block, F32),
        ),
        out_terms + in_terms + [w_out, w_in, cotangent],
    )
    grad_w_out, grad_w_in = sum_everywhere(local_out, local_in)
    out_terms, in_terms = propagate(grad_before, meta, own_tiles, other_tiles)
    grad_features = dense_call(
        functools.partial(end_kernel, len(out_terms)),
        jax.ShapeDtypeStruct(block, BF16),
        out_terms + in_terms + [w_out, w_in],
    )
    return activated, grad_features, grad_w_out, grad_w_in


def solution(mesh):
    placed = (
        P(("row", "col"), None),
        P(),
        P(),
        P("row", "col", None),
        P("row", "col"),
        P("row", "col", None, None, None),
        P(("row", "col"), None),
    )
    return jax.shard_map(
        local,
        mesh=mesh,
        in_specs=placed,
        out_specs=(P(("row", "col"), None), P(("row", "col"), None), P(), P()),
        check_vma=False,
    )
```

```python
import jax
import jax.numpy as jnp
from jax import lax
from jax.experimental import pallas as pl
from jax.experimental.pallas import tpu as pltpu
from jax.sharding import PartitionSpec as P

TILE = 256
LISTED = 16
F32 = jnp.float32
BF16 = jnp.bfloat16

ROWS = 32
COLS = 8


def moved(step):
    pairs = []
    for at in range(ROWS * COLS):
        r, c = at // COLS, at % COLS
        z, hi, core, lo, y = step(r // 4, r // 2 % 2, r % 2, c // 4, c % 4)
        pairs.append((at, (((z % 8) * 2 + hi) * 2 + core) * COLS + lo * 4 + y % 4))
    return pairs


def permute(x, step):
    return lax.ppermute(x, ("row", "col"), moved(step))


def swap_core(x):
    return permute(x, lambda z, hi, core, lo, y: (z, hi, 1 - core, lo, y))


def swap_hi(x):
    return permute(x, lambda z, hi, core, lo, y: (z, 1 - hi, core, lo, y))


def along_z(x):
    return permute(x, lambda z, hi, core, lo, y: (z + 1 - 2 * core, hi, core, lo, y))


def twice_along_z(x):
    return permute(x, lambda z, hi, core, lo, y: (z + 2 - 4 * core, hi, core, lo, y))


def along_y(x):
    return permute(x, lambda z, hi, core, lo, y: (z, hi, core, lo, y + 1 - 2 * core))


def across_y(x):
    return permute(x, lambda z, hi, core, lo, y: (z, hi, core, lo, y + 2))


def swap_lo(x):
    return permute(x, lambda z, hi, core, lo, y: (z, hi, core, 1 - lo, y))


def exchange_rows(x):
    return lax.all_to_all(x, "col", 0, 0, tiled=True)


def place():
    row, col = lax.axis_index("row"), lax.axis_index("col")
    return row >> 2, (row >> 1) & 1, row & 1, col >> 2, col & 3


def column_at(where, tile_col, forward):
    z, hi, core, _, _ = where
    dz = ((tile_col >> 2) - z) & 7
    j = jnp.where(core == (1 if forward else 0), dz, (8 - dz) & 7)
    k = (tile_col & 1) ^ core
    f = ((tile_col >> 1) & 1) ^ hi
    ends = jnp.logical_or(j == 0, j == 4)
    mine = jnp.logical_or(jnp.logical_and(j >= 1, j <= 3), jnp.logical_and(ends, k == 0))
    if forward:
        return mine, f + jnp.where(ends, 12 + (j >> 1), (j - 1) * 4 + k * 2)
    inner = jnp.where(j == 3, 10, (j - 1) * 4) + f * 2 + k
    return mine, jnp.where(j == 0, 8 + f, jnp.where(j == 4, 14 + f, inner))


def sum_row_at(where, which, tile_row):
    _, _, core, lo, y = where
    f = (tile_row >> 2) ^ lo
    dy = ((tile_row & 3) - y) & 3
    along = dy == 1 + 2 * core
    near = jnp.where(along, which * 2, 8 + (1 - which) * 2)
    return f + jnp.where(dy == 0, 6 + which * 8, jnp.where(dy == 2, 4 + which * 8, near))


ANYWHERE = pl.BlockSpec(memory_space=pl.ANY)
IN_HBM = pl.BlockSpec(memory_space=pltpu.HBM)
INTEGERS = pl.BlockSpec(memory_space=pltpu.SMEM)


def together(*arrays):
    return lax.optimization_barrier(arrays)


def tile_kernel(forward, sizes, *refs):
    slots, counts, tiles = refs[0:2], refs[2:4], refs[4:6]
    sources = refs[6 : 6 + len(sizes)]
    outs = refs[6 + len(sizes) : -6]
    rest, side, held, todo, side_sem, tile_sem = refs[-6:]
    sums, sent = outs[:2], outs[2:]
    where = place()

    copies = []
    first = 0
    for i, n in enumerate(sizes):
        copies.append(
            pltpu.make_async_copy(
                sources[i].at[:n, :TILE], side.at[first : first + n], side_sem.at[i]
            )
        )
        copies[-1].start()
        first += n

    def fetched(i):
        return pltpu.make_async_copy(tiles[0].at[0], held.at[i], tile_sem.at[i])

    n = 0
    for which in range(2):

        def note(k, n):
            slot = slots[which][0, 0, k]
            mine, col_at = column_at(where, slot & 31, forward)
            row_at = which * 8 + (slot >> 5)
            if forward:
                row_at = sum_row_at(where, which, slot >> 5)

            @pl.when(mine)
            def _():
                todo[0, n] = col_at if forward else row_at
                todo[1, n] = row_at if forward else col_at
                pltpu.make_async_copy(tiles[which].at[k], held.at[n], tile_sem.at[n]).start()

            return n + mine.astype(jnp.int32)

        n = lax.fori_loop(0, counts[which][0, 0], note, n)

    for x in (*sums, rest):
        x[...] = jnp.zeros_like(x)
    for copy in copies:
        copy.wait()

    def product(i, source):
        if forward:
            return jnp.dot(held[i], side[source], preferred_element_type=F32)
        return lax.dot_general(
            held[i], side[source], (((0,), (0,)), ((), ())), preferred_element_type=F32
        )

    def add_at(at, value):
        first = 0
        for x in (*sums, rest):
            last = first + x.shape[0]

            @pl.when(jnp.logical_and(at >= first, at < last))
            def _():
                x[at - first] += value

            first = last

    def pair(p, carry):
        i = 2 * p
        fetched(i).wait()
        whole = i + 1 < n

        @pl.when(whole)
        def _():
            fetched(i + 1).wait()

        j = jnp.where(whole, i + 1, i)
        a = product(i, todo[0, i])
        b = product(j, todo[0, j])
        add_at(todo[1, i], a)
        add_at(jnp.where(whole, todo[1, j], 16), b)
        return carry

    lax.fori_loop(0, (n + 1) >> 1, pair, 0)
    first = 0
    for out in sent:
        out[...] = rest[first : first + out.shape[0]].astype(BF16)
        first += out.shape[0]


def tile_call(forward, lists, sizes, sources):
    def kernel(*refs):
        tile_kernel(forward, sizes, *refs)

    vmem = pl.BlockSpec(memory_space=pltpu.VMEM)
    block = (TILE, TILE)
    kept, home, sent = (6, 2, (8,)) if forward else (8, 2, (4, 2))
    return pl.pallas_call(
        kernel,
        out_shape=[jax.ShapeDtypeStruct((n,) + block, F32) for n in (kept, home)]
        + [jax.ShapeDtypeStruct((n,) + block, BF16) for n in sent],
        in_specs=[INTEGERS] * 4 + [IN_HBM] + [ANYWHERE] * (1 + len(sources)),
        out_specs=[vmem] * (2 + len(sent)),
        scratch_shapes=[
            pltpu.VMEM((17 - kept - home,) + block, F32),
            pltpu.VMEM((16,) + block, BF16),
            pltpu.VMEM((2 * LISTED,) + block, BF16),
            pltpu.SMEM((2, 2 * LISTED), jnp.int32),
            pltpu.SemaphoreType.DMA((len(sources),)),
            pltpu.SemaphoreType.DMA((2 * LISTED,)),
        ],
        compiler_params=pltpu.CompilerParams(vmem_limit_bytes=24 * 2**20),
        cost_estimate=pl.CostEstimate(
            flops=16 * 2 * TILE**3,
            bytes_accessed=(100 if forward else 40) * 2**20,
            transcendentals=0,
        ),
    )(*lists, *sources)


def dot2(x, y, dims):
    high = x.astype(BF16)
    low = (x - high.astype(F32)).astype(BF16)
    return lax.dot_general(high, y, (dims, ((), ())), preferred_element_type=F32) + lax.dot_general(
        low, y, (dims, ((), ())), preferred_element_type=F32
    )


def fetch_all(pairs, sems):
    copies = [pltpu.make_async_copy(a, b, sems.at[i]) for i, (a, b) in enumerate(pairs)]
    for copy in copies:
        copy.start()
    for copy in copies:
        copy.wait()


def call_on_vmem(body, out_shape, *operands, arguments=()):
    operands = operands + tuple(arguments)
    arrays = [x[0] if isinstance(x, tuple) else x for x in operands]
    parts = [x[1] if isinstance(x, tuple) else None for x in operands]
    n = len(arrays)
    shapes = []
    for x, part in zip(arrays, parts):
        shape = x.shape if part is None else jax.eval_shape(lambda v, p=part: v[p], x).shape
        shapes.append(pltpu.VMEM(shape, x.dtype))

    def kernel(*refs):
        sources, outs, held, sems = refs[:n], refs[n : -n - 1], refs[-n - 1 : -1], refs[-1]
        views = [x if part is None else x.at[part] for x, part in zip(sources, parts)]
        fetch_all(list(zip(views, held)), sems)
        body(*held, *outs)

    vmem = pl.BlockSpec(memory_space=pltpu.VMEM)
    return pl.pallas_call(
        kernel,
        out_shape=out_shape,
        in_specs=[ANYWHERE] * (n - len(arguments)) + [IN_HBM] * len(arguments),
        out_specs=jax.tree.map(lambda _: vmem, out_shape),
        scratch_shapes=shapes + [pltpu.SemaphoreType.DMA((n,))],
        compiler_params=pltpu.CompilerParams(vmem_limit_bytes=16 * 2**20),
        cost_estimate=pl.CostEstimate(
            flops=8 * 2 * TILE**3, bytes_accessed=4 * 2**20, transcendentals=TILE * TILE
        ),
    )(*arrays)


N_ROW_TERMS, N_COL_TERMS = 6, 4


def sum_of(terms):
    total = terms[0][...].astype(F32)
    for term in terms[1:]:
        total = total + term[...].astype(F32)
    return total


def sums_of(terms):
    return sum_of(terms[:N_ROW_TERMS]), sum_of(terms[N_ROW_TERMS:])


def middle_body(*refs):
    out_sum, in_sum = sums_of(refs[: N_ROW_TERMS + N_COL_TERMS])
    w_out, w_in, cotangent, activated, grad_before, keep, give = refs[
        N_ROW_TERMS + N_COL_TERMS :
    ]
    before = dot2(out_sum, w_out[...], ((1,), (0,))) + dot2(in_sum, w_in[...], ((1,), (0,)))
    gate = jax.nn.sigmoid(before)
    activated[...] = (before * gate).astype(BF16)
    grad = (cotangent[...].astype(F32) * gate * (1.0 + before * (1.0 - gate))).astype(BF16)
    grad_before[...] = grad
    first = place()[2] == 0
    local_out = dot2(out_sum, grad, ((0,), (0,)))
    local_in = dot2(in_sum, grad, ((0,), (0,)))
    keep[...] = jnp.where(first, local_out, local_in)
    give[...] = jnp.where(first, local_in, local_out)


def end_body(*refs):
    back_forward, back_transposed = sums_of(refs[: N_ROW_TERMS + N_COL_TERMS])
    w_out, w_in, grad_features = refs[N_ROW_TERMS + N_COL_TERMS :]
    grad_features[...] = (
        dot2(back_transposed, w_out[...], ((1,), (1,)))
        + dot2(back_forward, w_in[...], ((1,), (1,)))
    ).astype(BF16)


def add(parts, *arrived):
    for x in arrived:
        parts = parts + x.astype(F32)
    return parts.astype(BF16)


class Nothing:
    def rows_out(self, source):
        return jnp.broadcast_to(source, (COLS, TILE, TILE))

    def rows_arrived(self, rows):
        pass

    def step(self, n):
        return ()

    def join(self):
        return ()


def two_terms(x):
    high = x.astype(BF16)
    return high, (x - high.astype(F32)).astype(BF16)


PIECE = TILE // COLS


class SumEverywhere:
    def __init__(self, keep, give):
        self.keep, self.give = keep, give
        self.moves = [
            swap_hi,
            self.flip_z(1),
            self.flip_z(2),
            self.flip_z(4),
        ]

    def flip_z(self, bit):
        return lambda x: permute(x, lambda z, hi, core, lo, y: (z ^ bit, hi, core, lo, y))

    def rows_out(self, source):
        def body(source, keep, given, out):
            for i in range(COLS):
                at = slice(i * PIECE, (i + 1) * PIECE)
                out[i, :TILE] = source[0]
                high, low = two_terms(keep[at] + given[at])
                out[i, TILE : TILE + PIECE] = high
                out[i, TILE + PIECE :] = low

        shape = jax.ShapeDtypeStruct((COLS, TILE + 2 * PIECE, TILE), BF16)
        return call_on_vmem(body, shape, source, self.keep, swap_core(self.give))

    def rows_arrived(self, rows):
        def body(part, out):
            total = part[0].astype(F32)
            for i in range(1, COLS):
                total = total + part[i].astype(F32)
            out[...] = total[:PIECE] + total[PIECE:]

        shape = jax.ShapeDtypeStruct((PIECE, TILE), F32)
        self.total = call_on_vmem(body, shape, (rows, (slice(None), slice(TILE, None))))

    def step(self, n):
        for _ in range(n):
            self.total = self.total + self.moves.pop(0)(self.total)
        return (self.total,)

    def join(self):
        self.mine = exchange_rows(jnp.broadcast_to(self.total, (COLS, PIECE, TILE)))
        return (self.mine,)

    def result(self):
        mine = self.mine.reshape(TILE, TILE)
        whole = jax.ShapeDtypeStruct((TILE, TILE), F32)
        return call_on_vmem(order_kernel, [whole] * 2, mine, swap_core(mine))


def order_kernel(mine, theirs, first, second):
    @pl.when(place()[2] == 0)
    def _():
        first[...] = mine[...]
        second[...] = theirs[...]

    @pl.when(place()[2] == 1)
    def _():
        first[...] = theirs[...]
        second[...] = mine[...]


def propagate(source, lists, early, beside):
    source = source[None]
    with jax.named_scope("gather"):
        from_hi = swap_hi(source)
        rows = beside.rows_out(source)
        rows, from_hi = together(rows, from_hi)
        rows = exchange_rows(rows)
        twin = swap_core(source)
        z0 = jnp.concatenate([source, from_hi, twin, swap_core(from_hi)])
        z1 = along_z(z0)
        z2 = along_z(z1)
        rows, z1, *_ = together(rows, z1, *early)
        rows_twin, z2 = together(swap_core(rows), z2)
        z3 = along_z(z2)
        z4 = twice_along_z(z2[:2])
        beside.rows_arrived(rows)

    with jax.named_scope("transposed"):
        kept, home, three, four = tile_call(False, lists, (8, 8), [rows, rows_twin])
        z3, z4, three, four = together(z3, z4, three, four)
        three = along_z(three)
        four = twice_along_z(four)

    with jax.named_scope("forward"):
        sources = [z1, z2, z3, z0, z4]
        sums, home_row, other = tile_call(True, lists, (4, 4, 4, 2, 2), sources)
        sums, home_row, other, three, four, *_ = together(
            sums, home_row, other, three, four, *beside.step(2)
        )
        other = swap_core(other)
        three = kept[4:8] + three.astype(F32)
        two = jnp.concatenate(
            [
                three[:1] + four[:1].astype(F32),
                three[1:2],
                three[2:3] + four[1:].astype(F32),
                three[3:],
            ]
        )
        two, other = together(two.astype(BF16), other)
        two = along_z(two)
        near = along_y(add(sums[:4], other[:4]))
        across = across_y(add(sums[4:], other[4:6]))

    with jax.named_scope("sums"):
        two, *_ = together(two, *beside.step(2))
        one_hi, one = together(add(kept[2:4], two[2:]), add(kept[:2], two[:2]))
        one_hi = along_z(one_hi)
        one = along_z(one)
        near, across, one_hi = together(near, across, one_hi)
        far = swap_hi(add(home[1:], one_hi[:1], swap_core(one_hi[1:])))
        near_twin = swap_core(near[2:])
        far_row = swap_lo(
            add(home_row[1:], other[7:], near[1:2], near_twin[1:], across[1:])
        )
        one, *_ = together(one, *beside.join())
        one_twin = swap_core(one[1:])
    return [
        (home_row, 0),
        (other, 6),
        (near, 0),
        (near_twin, 0),
        (across, 0),
        (far_row, 0),
        (home, 0),
        (one, 0),
        (one_twin, 0),
        (far, 0),
    ]


def local(features, w_out, w_in, tile_slot, tile_count, tile_values, cotangent):
    tiles = tile_values[0, 0]
    other = [swap_core(tile_slot), swap_core(tile_count), swap_core(tiles)]
    lists = [tile_slot, other[0], tile_count, other[1], tiles, other[2]]

    terms = propagate(features, lists, other[:2], Nothing())
    block = (TILE, TILE)
    activated, grad_before, keep, give = call_on_vmem(
        middle_body,
        [jax.ShapeDtypeStruct(block, dtype) for dtype in (BF16, BF16, F32, F32)],
        *terms,
        arguments=(w_out, w_in, cotangent),
    )
    weights = SumEverywhere(keep, give)
    terms = propagate(grad_before, lists, [], weights)
    with jax.named_scope("weights"):
        grad_w_out, grad_w_in = weights.result()
    grad_features = call_on_vmem(
        end_body, jax.ShapeDtypeStruct(block, BF16), *terms, arguments=(w_out, w_in)
    )
    return activated, grad_features, grad_w_out, grad_w_in


def solution(mesh):
    placed = (
        P(("row", "col"), None),
        P(),
        P(),
        P("row", "col", None),
        P("row", "col"),
        P("row", "col", None, None, None),
        P(("row", "col"), None),
    )
    return jax.shard_map(
        local,
        mesh=mesh,
        in_specs=placed,
        out_specs=(P(("row", "col"), None), P(("row", "col"), None), P(), P()),
        check_vma=False,
    )
```

```python
import jax
import jax.numpy as jnp
from jax import lax
from jax.experimental import pallas as pl
from jax.experimental.pallas import tpu as pltpu
from jax.sharding import PartitionSpec as P

TILE = 256
LISTED = 16
F32 = jnp.float32
BF16 = jnp.bfloat16

ROWS = 32
COLS = 8


def moved(step):
    pairs = []
    for at in range(ROWS * COLS):
        r, c = at // COLS, at % COLS
        z, hi, core, lo, y = step(r // 4, r // 2 % 2, r % 2, c // 4, c % 4)
        pairs.append((at, (((z % 8) * 2 + hi) * 2 + core) * COLS + lo * 4 + y % 4))
    return pairs


def permute(x, step):
    return lax.ppermute(x, ("row", "col"), moved(step))


def swap_core(x):
    return permute(x, lambda z, hi, core, lo, y: (z, hi, 1 - core, lo, y))


def swap_hi(x):
    return permute(x, lambda z, hi, core, lo, y: (z, 1 - hi, core, lo, y))


def along_z(x):
    return permute(x, lambda z, hi, core, lo, y: (z + 1 - 2 * core, hi, core, lo, y))


def twice_along_z(x):
    return permute(x, lambda z, hi, core, lo, y: (z + 2 - 4 * core, hi, core, lo, y))


def along_z_to_hi(x):
    return permute(x, lambda z, hi, core, lo, y: (z + 1 - 2 * core, 1 - hi, core, lo, y))


def along_y_to_lo(x):
    return permute(x, lambda z, hi, core, lo, y: (z, hi, core, 1 - lo, y + 1 - 2 * core))


def across_y_to_lo(x):
    return permute(x, lambda z, hi, core, lo, y: (z, hi, core, 1 - lo, y + 2))


def along_y(x):
    return permute(x, lambda z, hi, core, lo, y: (z, hi, core, lo, y + 1 - 2 * core))


def across_y(x):
    return permute(x, lambda z, hi, core, lo, y: (z, hi, core, lo, y + 2))


def swap_lo(x):
    return permute(x, lambda z, hi, core, lo, y: (z, hi, core, 1 - lo, y))


def exchange_rows(x):
    return lax.all_to_all(x, "col", 0, 0, tiled=True)


def place():
    row, col = lax.axis_index("row"), lax.axis_index("col")
    return row >> 2, (row >> 1) & 1, row & 1, col >> 2, col & 3


def column_at(where, tile_col, forward):
    z, hi, core, _, _ = where
    dz = ((tile_col >> 2) - z) & 7
    j = jnp.where(core == (1 if forward else 0), dz, (8 - dz) & 7)
    k = (tile_col & 1) ^ core
    f = ((tile_col >> 1) & 1) ^ hi
    ends = jnp.logical_or(j == 0, j == 4)
    mine = jnp.logical_or(jnp.logical_and(j >= 1, j <= 3), jnp.logical_and(ends, k == 0))
    if forward:
        return mine, f + jnp.where(ends, 12 + (j >> 1), (j - 1) * 4 + k * 2)
    inner = jnp.where(j == 3, 9, (j - 1) * 4) + f * 2 + k
    return mine, jnp.where(j == 0, 8 + f * 7, jnp.where(j == 4, 13 + f, inner))


def sum_row_at(where, which, tile_row):
    _, _, core, lo, y = where
    f = (tile_row >> 2) ^ lo
    dy = ((tile_row & 3) - y) & 3
    along = dy == 1 + 2 * core
    near = f * 2 + jnp.where(along, which, 8 + 1 - which)
    return jnp.where(dy == 0, 6 + f + which * 8, jnp.where(dy == 2, 4 + f + which * 8, near))


ANYWHERE = pl.BlockSpec(memory_space=pl.ANY)
IN_HBM = pl.BlockSpec(memory_space=pltpu.HBM)
INTEGERS = pl.BlockSpec(memory_space=pltpu.SMEM)


def together(*arrays):
    return lax.optimization_barrier(arrays)


def tile_kernel(forward, sizes, *refs):
    slots, counts, tiles = refs[0:2], refs[2:4], refs[4:6]
    sources = refs[6 : 6 + len(sizes)]
    outs = refs[6 + len(sizes) : -6]
    rest, side, held, todo, side_sem, tile_sem = refs[-6:]
    sums, sent = outs[:2], outs[2:]
    where = place()

    copies = []
    first = 0
    for i, n in enumerate(sizes):
        copies.append(
            pltpu.make_async_copy(
                sources[i].at[:n, :TILE], side.at[first : first + n], side_sem.at[i]
            )
        )
        copies[-1].start()
        first += n

    def fetched(i):
        return pltpu.make_async_copy(tiles[0].at[0], held.at[i], tile_sem.at[i])

    n = 0
    for which in range(2):

        def note(k, n):
            slot = slots[which][0, 0, k]
            mine, col_at = column_at(where, slot & 31, forward)
            row_at = which * 8 + (slot >> 5)
            if forward:
                row_at = sum_row_at(where, which, slot >> 5)

            @pl.when(mine)
            def _():
                todo[0, n] = col_at if forward else row_at
                todo[1, n] = row_at if forward else col_at
                pltpu.make_async_copy(tiles[which].at[k], held.at[n], tile_sem.at[n]).start()

            return n + mine.astype(jnp.int32)

        n = lax.fori_loop(0, counts[which][0, 0], note, n)

    for x in (*sums, rest):
        x[...] = jnp.zeros_like(x)
    for copy in copies:
        copy.wait()

    def product(i, source):
        if forward:
            return jnp.dot(held[i], side[source], preferred_element_type=F32)
        return lax.dot_general(
            held[i], side[source], (((0,), (0,)), ((), ())), preferred_element_type=F32
        )

    def add_at(at, value):
        first = 0
        for x in (*sums, rest):
            last = first + x.shape[0]

            @pl.when(jnp.logical_and(at >= first, at < last))
            def _():
                x[at - first] += value

            first = last

    def pair(p, carry):
        i = 2 * p
        fetched(i).wait()
        whole = i + 1 < n

        @pl.when(whole)
        def _():
            fetched(i + 1).wait()

        j = jnp.where(whole, i + 1, i)
        a = product(i, todo[0, i])
        b = product(j, todo[0, j])
        add_at(todo[1, i], a)
        add_at(jnp.where(whole, todo[1, j], 16), b)
        return carry

    lax.fori_loop(0, (n + 1) >> 1, pair, 0)
    first = 0
    for out in sent:
        out[...] = rest[first : first + out.shape[0]].astype(BF16)
        first += out.shape[0]


def tile_call(forward, lists, sizes, sources):
    def kernel(*refs):
        tile_kernel(forward, sizes, *refs)

    vmem = pl.BlockSpec(memory_space=pltpu.VMEM)
    block = (TILE, TILE)
    kept, home, sent = (6, 2, (8,)) if forward else (8, 1, (4, 2, 1))
    return pl.pallas_call(
        kernel,
        out_shape=[jax.ShapeDtypeStruct((n,) + block, F32) for n in (kept, home)]
        + [jax.ShapeDtypeStruct((n,) + block, BF16) for n in sent],
        in_specs=[INTEGERS] * 4 + [IN_HBM] + [ANYWHERE] * (1 + len(sources)),
        out_specs=[vmem] * (2 + len(sent)),
        scratch_shapes=[
            pltpu.VMEM((17 - kept - home,) + block, F32),
            pltpu.VMEM((16,) + block, BF16),
            pltpu.VMEM((2 * LISTED,) + block, BF16),
            pltpu.SMEM((2, 2 * LISTED), jnp.int32),
            pltpu.SemaphoreType.DMA((len(sources),)),
            pltpu.SemaphoreType.DMA((2 * LISTED,)),
        ],
        compiler_params=pltpu.CompilerParams(vmem_limit_bytes=24 * 2**20),
        cost_estimate=pl.CostEstimate(
            flops=16 * 2 * TILE**3,
            bytes_accessed=(100 if forward else 40) * 2**20,
            transcendentals=0,
        ),
    )(*lists, *sources)


def dot2(x, y, dims):
    high = x.astype(BF16)
    low = (x - high.astype(F32)).astype(BF16)
    return lax.dot_general(high, y, (dims, ((), ())), preferred_element_type=F32) + lax.dot_general(
        low, y, (dims, ((), ())), preferred_element_type=F32
    )


def fetch_all(pairs, sems):
    copies = [pltpu.make_async_copy(a, b, sems.at[i]) for i, (a, b) in enumerate(pairs)]
    for copy in copies:
        copy.start()
    for copy in copies:
        copy.wait()


def call_on_vmem(body, out_shape, *operands, arguments=()):
    operands = operands + tuple(arguments)
    arrays = [x[0] if isinstance(x, tuple) else x for x in operands]
    parts = [x[1] if isinstance(x, tuple) else None for x in operands]
    n = len(arrays)
    shapes = []
    for x, part in zip(arrays, parts):
        shape = x.shape if part is None else jax.eval_shape(lambda v, p=part: v[p], x).shape
        shapes.append(pltpu.VMEM(shape, x.dtype))

    def kernel(*refs):
        sources, outs, held, sems = refs[:n], refs[n : -n - 1], refs[-n - 1 : -1], refs[-1]
        views = [x if part is None else x.at[part] for x, part in zip(sources, parts)]
        fetch_all(list(zip(views, held)), sems)
        body(*held, *outs)

    vmem = pl.BlockSpec(memory_space=pltpu.VMEM)
    return pl.pallas_call(
        kernel,
        out_shape=out_shape,
        in_specs=[ANYWHERE] * (n - len(arguments)) + [IN_HBM] * len(arguments),
        out_specs=jax.tree.map(lambda _: vmem, out_shape),
        scratch_shapes=shapes + [pltpu.SemaphoreType.DMA((n,))],
        compiler_params=pltpu.CompilerParams(vmem_limit_bytes=16 * 2**20),
        cost_estimate=pl.CostEstimate(
            flops=8 * 2 * TILE**3, bytes_accessed=4 * 2**20, transcendentals=TILE * TILE
        ),
    )(*arrays)


N_ROW_TERMS, N_COL_TERMS = 9, 6


def sum_of(terms):
    total = terms[0][...].astype(F32)
    for term in terms[1:]:
        total = total + term[...].astype(F32)
    return total


def sums_of(terms):
    return sum_of(terms[:N_ROW_TERMS]), sum_of(terms[N_ROW_TERMS:])


def middle_body(*refs):
    out_sum, in_sum = sums_of(refs[: N_ROW_TERMS + N_COL_TERMS])
    w_out, w_in, cotangent, activated, grad_before, keep, give = refs[
        N_ROW_TERMS + N_COL_TERMS :
    ]
    before = dot2(out_sum, w_out[...], ((1,), (0,))) + dot2(in_sum, w_in[...], ((1,), (0,)))
    gate = jax.nn.sigmoid(before)
    activated[...] = (before * gate).astype(BF16)
    grad = (cotangent[...].astype(F32) * gate * (1.0 + before * (1.0 - gate))).astype(BF16)
    grad_before[...] = grad
    first = place()[2] == 0
    local_out = dot2(out_sum, grad, ((0,), (0,)))
    local_in = dot2(in_sum, grad, ((0,), (0,)))
    keep[...] = jnp.where(first, local_out, local_in)
    give[...] = jnp.where(first, local_in, local_out)


def end_body(*refs):
    back_forward, back_transposed = sums_of(refs[: N_ROW_TERMS + N_COL_TERMS])
    w_out, w_in, grad_features = refs[N_ROW_TERMS + N_COL_TERMS :]
    grad_features[...] = (
        dot2(back_transposed, w_out[...], ((1,), (1,)))
        + dot2(back_forward, w_in[...], ((1,), (1,)))
    ).astype(BF16)


def add(parts, *arrived):
    for x in arrived:
        parts = parts + x.astype(F32)
    return parts.astype(BF16)


class Nothing:
    def rows_out(self, source):
        def body(source, out):
            for i in range(COLS):
                out[i] = source[0]

        return call_on_vmem(body, jax.ShapeDtypeStruct((COLS, TILE, TILE), BF16), source)

    def rows_arrived(self, rows):
        pass

    def send(self):
        return ()

    def take(self, arrived):
        pass

    def join(self, *after):
        pass


def two_terms(x):
    high = x.astype(BF16)
    return high, (x - high.astype(F32)).astype(BF16)


PIECE = TILE // COLS


class SumEverywhere:
    def __init__(self, keep, give):
        self.keep, self.give = keep, give
        self.moves = [
            swap_hi,
            self.flip_z(1),
            self.flip_z(2),
            self.flip_z(4),
        ]

    def flip_z(self, bit):
        return lambda x: permute(x, lambda z, hi, core, lo, y: (z ^ bit, hi, core, lo, y))

    def rows_out(self, source):
        def body(source, keep, given, out):
            for i in range(COLS):
                at = slice(i * PIECE, (i + 1) * PIECE)
                out[i, :TILE] = source[0]
                high, low = two_terms(keep[at] + given[at])
                out[i, TILE : TILE + PIECE] = high
                out[i, TILE + PIECE :] = low

        shape = jax.ShapeDtypeStruct((COLS, TILE + 2 * PIECE, TILE), BF16)
        return call_on_vmem(body, shape, source, self.keep, swap_core(self.give))

    def rows_arrived(self, rows):
        def body(part, out):
            total = part[0].astype(F32)
            for i in range(1, COLS):
                total = total + part[i].astype(F32)
            out[...] = total[:PIECE] + total[PIECE:]

        shape = jax.ShapeDtypeStruct((PIECE, TILE), F32)
        self.total = call_on_vmem(body, shape, (rows, (slice(None), slice(TILE, None))))

    def send(self):
        with jax.named_scope("weights"):
            return (self.moves.pop(0)(self.total),)

    def take(self, arrived):
        with jax.named_scope("weights"):
            self.total = self.total + arrived[0]

    def join(self, *after):
        total, *_ = together(self.total, *after)
        self.mine = exchange_rows(jnp.broadcast_to(total, (COLS, PIECE, TILE)))

    def result(self):
        mine = self.mine.reshape(TILE, TILE)
        whole = jax.ShapeDtypeStruct((TILE, TILE), F32)
        return call_on_vmem(order_kernel, [whole] * 2, mine, swap_core(mine))


def order_kernel(mine, theirs, first, second):
    @pl.when(place()[2] == 0)
    def _():
        first[...] = mine[...]
        second[...] = theirs[...]

    @pl.when(place()[2] == 1)
    def _():
        first[...] = theirs[...]
        second[...] = mine[...]


def propagate(source, lists, early, beside):
    source = source[None]
    with jax.named_scope("gather"):
        from_hi = swap_hi(source)
        rows = beside.rows_out(source)
        rows, from_hi = together(rows, from_hi)
        rows = exchange_rows(rows)
        twin = swap_core(source)
        z0 = jnp.concatenate([source, from_hi, twin, swap_core(from_hi)])
        z1 = along_z(z0)
        z2 = along_z(z1)
        rows, z1, *_ = together(rows, z1, *early)
        beside.rows_arrived(rows)
        rows_twin, z2, *sent = together(swap_core(rows), z2, *beside.send())
        beside.take(sent)
        z3 = along_z(z2)
        z4 = twice_along_z(z2[:2])

    with jax.named_scope("transposed"):
        kept, home, three, four, home_hi = tile_call(False, lists, (8, 8), [rows, rows_twin])
        z3, z4, three, four, *sent = together(z3, z4, three, four, *beside.send())
        beside.take(sent)
        three = along_z(three)
        four = twice_along_z(four)

    with jax.named_scope("forward"):
        sources = [z1, z2, z3, z0, z4]
        sums, home_row, other = tile_call(True, lists, (4, 4, 4, 2, 2), sources)
        other = swap_core(other)
        sums, three, four, *sent = together(sums, three, four, *beside.send())
        beside.take(sent)
        three = kept[4:8] + three.astype(F32)
        two = jnp.concatenate(
            [
                three[:1] + four[:1].astype(F32),
                three[1:2],
                three[2:3] + four[1:].astype(F32),
                three[3:],
            ]
        )
        two = along_z(two.astype(BF16))
        home_hi = swap_hi(home_hi)
        near = along_y(add(sums[:2], other[:2]))
        near_lo = along_y_to_lo(add(sums[2:4], other[2:4]))
        across = across_y(add(sums[4:5], other[4:5]))
        across_lo = across_y_to_lo(add(sums[5:6], other[5:6]))
        home_lo = swap_lo(add(home_row[1:], other[7:]))

    with jax.named_scope("sums"):
        two, home_hi, *sent = together(two, home_hi, *beside.send())
        beside.take(sent)
        one_hi, one = together(add(kept[2:4], two[2:]), add(kept[:2], two[:2]))
        one_hi = along_z_to_hi(one_hi)
        one = along_z(one)
        beside.join(near, near_lo)
    return [
        (home_row, 0),
        (other, 6),
        (near, 0),
        (swap_core(near[1:]), 0),
        (near_lo, 0),
        (swap_core(near_lo[1:]), 0),
        (across, 0),
        (across_lo, 0),
        (home_lo, 0),
        (home, 0),
        (one, 0),
        (swap_core(one[1:]), 0),
        (one_hi, 0),
        (swap_core(one_hi[1:]), 0),
        (home_hi, 0),
    ]


def local(features, w_out, w_in, tile_slot, tile_count, tile_values, cotangent):
    tiles = tile_values[0, 0]
    other = [swap_core(tile_slot), swap_core(tile_count), swap_core(tiles)]
    lists = [tile_slot, other[0], tile_count, other[1], tiles, other[2]]

    terms = propagate(features, lists, other[:2], Nothing())
    block = (TILE, TILE)
    activated, grad_before, keep, give = call_on_vmem(
        middle_body,
        [jax.ShapeDtypeStruct(block, dtype) for dtype in (BF16, BF16, F32, F32)],
        *terms,
        arguments=(w_out, w_in, cotangent),
    )
    weights = SumEverywhere(keep, give)
    terms = propagate(grad_before, lists, [], weights)
    with jax.named_scope("weights"):
        grad_w_out, grad_w_in = weights.result()
    grad_features = call_on_vmem(
        end_body, jax.ShapeDtypeStruct(block, BF16), *terms, arguments=(w_out, w_in)
    )
    return activated, grad_features, grad_w_out, grad_w_in


def solution(mesh):
    placed = (
        P(("row", "col"), None),
        P(),
        P(),
        P("row", "col", None),
        P("row", "col"),
        P("row", "col", None, None, None),
        P(("row", "col"), None),
    )
    return jax.shard_map(
        local,
        mesh=mesh,
        in_specs=placed,
        out_specs=(P(("row", "col"), None), P(("row", "col"), None), P(), P()),
        check_vma=False,
    )
```

```python
import jax
import jax.numpy as jnp
from jax import lax
from jax.experimental import pallas as pl
from jax.experimental.pallas import tpu as pltpu
from jax.sharding import PartitionSpec as P

TILE = 256
LISTED = 16
F32 = jnp.float32
BF16 = jnp.bfloat16

ROWS = 32
COLS = 8


def moved(step):
    pairs = []
    for at in range(ROWS * COLS):
        r, c = at // COLS, at % COLS
        z, hi, core, lo, y = step(r // 4, r // 2 % 2, r % 2, c // 4, c % 4)
        pairs.append((at, (((z % 8) * 2 + hi) * 2 + core) * COLS + lo * 4 + y % 4))
    return pairs


def permute(x, step):
    return lax.ppermute(x, ("row", "col"), moved(step))


def swap_core(x):
    return permute(x, lambda z, hi, core, lo, y: (z, hi, 1 - core, lo, y))


def swap_hi(x):
    return permute(x, lambda z, hi, core, lo, y: (z, 1 - hi, core, lo, y))


def along_z(x):
    return permute(x, lambda z, hi, core, lo, y: (z + 1 - 2 * core, hi, core, lo, y))


def twice_along_z(x):
    return permute(x, lambda z, hi, core, lo, y: (z + 2 - 4 * core, hi, core, lo, y))


def along_z_to_hi(x):
    return permute(x, lambda z, hi, core, lo, y: (z + 1 - 2 * core, 1 - hi, core, lo, y))


def along_y_to_lo(x):
    return permute(x, lambda z, hi, core, lo, y: (z, hi, core, 1 - lo, y + 1 - 2 * core))


def across_y_to_lo(x):
    return permute(x, lambda z, hi, core, lo, y: (z, hi, core, 1 - lo, y + 2))


def along_y(x):
    return permute(x, lambda z, hi, core, lo, y: (z, hi, core, lo, y + 1 - 2 * core))


def across_y(x):
    return permute(x, lambda z, hi, core, lo, y: (z, hi, core, lo, y + 2))


def swap_lo(x):
    return permute(x, lambda z, hi, core, lo, y: (z, hi, core, 1 - lo, y))


def exchange_rows(x):
    return lax.all_to_all(x, "col", 0, 0, tiled=True)


def place():
    row, col = lax.axis_index("row"), lax.axis_index("col")
    return row >> 2, (row >> 1) & 1, row & 1, col >> 2, col & 3


def column_at(where, tile_col, forward):
    z, hi, core, _, _ = where
    dz = ((tile_col >> 2) - z) & 7
    j = jnp.where(core == (1 if forward else 0), dz, (8 - dz) & 7)
    k = (tile_col & 1) ^ core
    f = ((tile_col >> 1) & 1) ^ hi
    ends = jnp.logical_or(j == 0, j == 4)
    mine = jnp.logical_or(jnp.logical_and(j >= 1, j <= 3), jnp.logical_and(ends, k == 0))
    if forward:
        return mine, f + jnp.where(ends, 12 + (j >> 1), (j - 1) * 4 + k * 2)
    inner = jnp.where(j == 3, 9, (j - 1) * 4) + f * 2 + k
    return mine, jnp.where(j == 0, 8 + f * 7, jnp.where(j == 4, 13 + f, inner))


def sum_row_at(where, which, tile_row):
    _, _, core, lo, y = where
    f = (tile_row >> 2) ^ lo
    dy = ((tile_row & 3) - y) & 3
    along = dy == 1 + 2 * core
    near = f * 2 + jnp.where(along, which, 8 + 1 - which)
    return jnp.where(dy == 0, 6 + f + which * 8, jnp.where(dy == 2, 4 + f + which * 8, near))


ANYWHERE = pl.BlockSpec(memory_space=pl.ANY)
IN_HBM = pl.BlockSpec(memory_space=pltpu.HBM)
INTEGERS = pl.BlockSpec(memory_space=pltpu.SMEM)


def together(*arrays):
    return lax.optimization_barrier(arrays)


def tile_kernel(forward, sizes, *refs):
    slots, counts, tiles = refs[0:2], refs[2:4], refs[4:6]
    sources = refs[6 : 6 + len(sizes)]
    outs = refs[6 + len(sizes) : -3]
    total, side, todo = refs[-3:]
    where = place()

    counted = []
    for which in range(2):

        def note(k, n):
            slot = slots[which][0, 0, k]
            mine, col_at = column_at(where, slot & 31, forward)
            row_at = slot >> 5
            if forward:
                row_at = sum_row_at(where, which, slot >> 5)

            @pl.when(mine)
            def _():
                todo[which, 0, n] = k
                todo[which, 1, n] = col_at if forward else row_at
                todo[which, 2, n] = row_at if forward else col_at

            return n + mine.astype(jnp.int32)

        counted.append(lax.fori_loop(0, counts[which][0, 0], note, 0))

    total[...] = jnp.zeros_like(total)
    if forward:
        first = 0
        for source, n in zip(sources, sizes):
            side[first : first + n] = source[:n]
            first += n

    def product(which, tile, at):
        if forward:
            return jnp.dot(tile, side[at], preferred_element_type=F32)
        return lax.dot_general(
            tile,
            sources[which][at, :TILE],
            (((0,), (0,)), ((), ())),
            preferred_element_type=F32,
        )

    for which in range(2):
        n = counted[which]

        def step(p, carry):
            products = []
            for u in range(2):
                i = 2 * p + u
                real = i < n
                i = jnp.where(real, i, 2 * p)
                value = product(which, tiles[which][todo[which, 0, i]], todo[which, 1, i])
                products.append((jnp.where(real, todo[which, 2, i], 16), value))
            for at, value in products:
                total[at] += value
            return carry

        lax.fori_loop(0, (n + 1) >> 1, step, 0)
    first = 0
    for out in outs:
        out[...] = total[first : first + out.shape[0]].astype(out.dtype)
        first += out.shape[0]


def tile_call(forward, lists, sizes, sources):
    def kernel(*refs):
        tile_kernel(forward, sizes, *refs)

    vmem = pl.BlockSpec(memory_space=pltpu.VMEM)
    block = (TILE, TILE)
    kept, home, sent = (6, 2, (8,)) if forward else (8, 1, (4, 2, 1))
    return pl.pallas_call(
        kernel,
        out_shape=[jax.ShapeDtypeStruct((n,) + block, F32) for n in (kept, home)]
        + [jax.ShapeDtypeStruct((n,) + block, BF16) for n in sent],
        in_specs=[INTEGERS] * 4 + [vmem] * (2 + len(sources)),
        out_specs=[vmem] * (2 + len(sent)),
        scratch_shapes=[
            pltpu.VMEM((17,) + block, F32),
            pltpu.VMEM((16,) + block, BF16),
            pltpu.SMEM((2, 3, LISTED), jnp.int32),
        ],
        compiler_params=pltpu.CompilerParams(vmem_limit_bytes=24 * 2**20),
        cost_estimate=pl.CostEstimate(
            flops=16 * 2 * TILE**3,
            bytes_accessed=(100 if forward else 40) * 2**20,
            transcendentals=0,
        ),
    )(*lists, *sources)


def dot2(x, y, dims):
    high = x.astype(BF16)
    low = (x - high.astype(F32)).astype(BF16)
    return lax.dot_general(high, y, (dims, ((), ())), preferred_element_type=F32) + lax.dot_general(
        low, y, (dims, ((), ())), preferred_element_type=F32
    )


def fetch_all(pairs, sems):
    copies = [pltpu.make_async_copy(a, b, sems.at[i]) for i, (a, b) in enumerate(pairs)]
    for copy in copies:
        copy.start()
    for copy in copies:
        copy.wait()


def call_on_vmem(body, out_shape, *operands, arguments=()):
    operands = operands + tuple(arguments)
    arrays = [x[0] if isinstance(x, tuple) else x for x in operands]
    parts = [x[1] if isinstance(x, tuple) else None for x in operands]
    n, first_argument = len(arrays), len(arrays) - len(arguments)
    copied = []
    for i, (x, part) in enumerate(zip(arrays, parts)):
        if i >= first_argument or (part is not None and x.shape[0] > 2):
            copied.append(i)
    shapes = []
    for i in copied:
        x, part = arrays[i], parts[i]
        shape = x.shape if part is None else jax.eval_shape(lambda v, p=part: v[p], x).shape
        shapes.append(pltpu.VMEM(shape, x.dtype))

    def kernel(*refs):
        sources, outs = list(refs[:n]), refs[n : len(refs) - len(copied) - 1]
        held, sems = refs[len(refs) - len(copied) - 1 : -1], refs[-1]
        pairs = []
        for i, to in zip(copied, held):
            pairs.append((sources[i] if parts[i] is None else sources[i].at[parts[i]], to))
        fetch_all(pairs, sems)
        for i, to in zip(copied, held):
            sources[i] = to
        for i, part in enumerate(parts):
            if part is not None and i not in copied:
                sources[i] = sources[i].at[part]
        body(*sources, *outs)

    vmem = pl.BlockSpec(memory_space=pltpu.VMEM)
    specs = []
    for i in range(n):
        specs.append(IN_HBM if i >= first_argument else ANYWHERE if i in copied else vmem)
    return pl.pallas_call(
        kernel,
        out_shape=out_shape,
        in_specs=specs,
        out_specs=jax.tree.map(lambda _: vmem, out_shape),
        scratch_shapes=shapes + [pltpu.SemaphoreType.DMA((max(len(copied), 1),))],
        compiler_params=pltpu.CompilerParams(vmem_limit_bytes=16 * 2**20),
        cost_estimate=pl.CostEstimate(
            flops=8 * 2 * TILE**3, bytes_accessed=4 * 2**20, transcendentals=TILE * TILE
        ),
    )(*arrays)


N_ROW_TERMS, N_COL_TERMS = 9, 6


def sum_of(terms):
    total = terms[0][...].astype(F32)
    for term in terms[1:]:
        total = total + term[...].astype(F32)
    return total


def sums_of(terms):
    return sum_of(terms[:N_ROW_TERMS]), sum_of(terms[N_ROW_TERMS:])


def middle_body(*refs):
    out_sum, in_sum = sums_of(refs[: N_ROW_TERMS + N_COL_TERMS])
    w_out, w_in, cotangent, activated, grad_before, keep, give = refs[
        N_ROW_TERMS + N_COL_TERMS :
    ]
    before = dot2(out_sum, w_out[...], ((1,), (0,))) + dot2(in_sum, w_in[...], ((1,), (0,)))
    gate = jax.nn.sigmoid(before)
    activated[...] = (before * gate).astype(BF16)
    grad = (cotangent[...].astype(F32) * gate * (1.0 + before * (1.0 - gate))).astype(BF16)
    grad_before[...] = grad
    first = place()[2] == 0
    local_out = dot2(out_sum, grad, ((0,), (0,)))
    local_in = dot2(in_sum, grad, ((0,), (0,)))
    keep[...] = jnp.where(first, local_out, local_in)
    give[...] = jnp.where(first, local_in, local_out)


def end_body(*refs):
    back_forward, back_transposed = sums_of(refs[: N_ROW_TERMS + N_COL_TERMS])
    w_out, w_in, grad_features = refs[N_ROW_TERMS + N_COL_TERMS :]
    grad_features[...] = (
        dot2(back_transposed, w_out[...], ((1,), (1,)))
        + dot2(back_forward, w_in[...], ((1,), (1,)))
    ).astype(BF16)


def add(parts, *arrived):
    for x in arrived:
        parts = parts + x.astype(F32)
    return parts.astype(BF16)


class Nothing:
    def rows_out(self, source):
        def body(source, out):
            for i in range(COLS):
                out[i] = source[0]

        return call_on_vmem(body, jax.ShapeDtypeStruct((COLS, TILE, TILE), BF16), source)

    def rows_arrived(self, rows):
        pass

    def send(self):
        return ()

    def take(self, arrived):
        pass

    def join(self, *after):
        pass


def two_terms(x):
    high = x.astype(BF16)
    return high, (x - high.astype(F32)).astype(BF16)


PIECE = TILE // COLS


class SumEverywhere:
    def __init__(self, keep, give):
        self.keep, self.give = keep, give
        self.moves = [
            swap_hi,
            self.flip_z(1),
            self.flip_z(2),
            self.flip_z(4),
        ]

    def flip_z(self, bit):
        return lambda x: permute(x, lambda z, hi, core, lo, y: (z ^ bit, hi, core, lo, y))

    def rows_out(self, source):
        def body(source, keep, given, out):
            for i in range(COLS):
                at = slice(i * PIECE, (i + 1) * PIECE)
                out[i, :TILE] = source[0]
                high, low = two_terms(keep[at] + given[at])
                out[i, TILE : TILE + PIECE] = high
                out[i, TILE + PIECE :] = low

        shape = jax.ShapeDtypeStruct((COLS, TILE + 2 * PIECE, TILE), BF16)
        return call_on_vmem(body, shape, source, self.keep, swap_core(self.give))

    def rows_arrived(self, rows):
        def body(part, out):
            total = part[0].astype(F32)
            for i in range(1, COLS):
                total = total + part[i].astype(F32)
            out[...] = total[:PIECE] + total[PIECE:]

        shape = jax.ShapeDtypeStruct((PIECE, TILE), F32)
        self.total = call_on_vmem(body, shape, (rows, (slice(None), slice(TILE, None))))

    def send(self):
        with jax.named_scope("weights"):
            return (self.moves.pop(0)(self.total),)

    def take(self, arrived):
        with jax.named_scope("weights"):
            self.total = self.total + arrived[0]

    def join(self, *after):
        total, *_ = together(self.total, *after)
        self.mine = exchange_rows(jnp.broadcast_to(total, (COLS, PIECE, TILE)))

    def result(self):
        mine = self.mine.reshape(TILE, TILE)
        whole = jax.ShapeDtypeStruct((TILE, TILE), F32)
        return call_on_vmem(order_kernel, [whole] * 2, mine, swap_core(mine))


def order_kernel(mine, theirs, first, second):
    @pl.when(place()[2] == 0)
    def _():
        first[...] = mine[...]
        second[...] = theirs[...]

    @pl.when(place()[2] == 1)
    def _():
        first[...] = theirs[...]
        second[...] = mine[...]


def propagate(source, lists, early, beside):
    source = source[None]
    with jax.named_scope("gather"):
        from_hi = swap_hi(source)
        rows = beside.rows_out(source)
        rows, from_hi = together(rows, from_hi)
        rows = exchange_rows(rows)
        twin = swap_core(source)
        z0 = jnp.concatenate([source, from_hi, twin, swap_core(from_hi)])
        z1 = along_z(z0)
        z2 = along_z(z1)
        rows, z1, *_ = together(rows, z1, *early)
        beside.rows_arrived(rows)
        rows_twin, z2, *sent = together(swap_core(rows), z2, *beside.send())
        beside.take(sent)
        z3 = along_z(z2)
        z4 = twice_along_z(z2[:2])

    with jax.named_scope("transposed"):
        kept, home, three, four, home_hi = tile_call(False, lists, (8, 8), [rows, rows_twin])
        z3, z4, three, four, *sent = together(z3, z4, three, four, *beside.send())
        beside.take(sent)
        three = along_z(three)
        four = twice_along_z(four)

    with jax.named_scope("forward"):
        sources = [z1, z2, z3, z0, z4]
        sums, home_row, other = tile_call(True, lists, (4, 4, 4, 2, 2), sources)
        other = swap_core(other)
        sums, three, four, *sent = together(sums, three, four, *beside.send())
        beside.take(sent)
        three = kept[4:8] + three.astype(F32)
        two = jnp.concatenate(
            [
                three[:1] + four[:1].astype(F32),
                three[1:2],
                three[2:3] + four[1:].astype(F32),
                three[3:],
            ]
        )
        two = along_z(two.astype(BF16))
        home_hi = swap_hi(home_hi)
        near = along_y(add(sums[:2], other[:2]))
        near_lo = along_y_to_lo(add(sums[2:4], other[2:4]))
        across = across_y(add(sums[4:5], other[4:5]))
        across_lo = across_y_to_lo(add(sums[5:6], other[5:6]))
        home_lo = swap_lo(add(home_row[1:], other[7:]))

    with jax.named_scope("sums"):
        two, near, near_lo, home_hi, *sent = together(
            two, near, near_lo, home_hi, *beside.send()
        )
        beside.take(sent)
        one_hi, one = together(add(kept[2:4], two[2:]), add(kept[:2], two[:2]))
        one_hi = along_z_to_hi(one_hi)
        one = along_z(one)
        beside.join(near, near_lo)
    return [
        (home_row, 0),
        (other, 6),
        (near, 0),
        (swap_core(near[1:]), 0),
        (near_lo, 0),
        (swap_core(near_lo[1:]), 0),
        (across, 0),
        (across_lo, 0),
        (home_lo, 0),
        (home, 0),
        (one, 0),
        (swap_core(one[1:]), 0),
        (one_hi, 0),
        (swap_core(one_hi[1:]), 0),
        (home_hi, 0),
    ]


def local(features, w_out, w_in, tile_slot, tile_count, tile_values, cotangent):
    tiles = tile_values[0, 0]
    other = [swap_core(tile_slot), swap_core(tile_count), swap_core(tiles)]
    lists = [tile_slot, other[0], tile_count, other[1], tiles, other[2]]

    terms = propagate(features, lists, other[:2], Nothing())
    block = (TILE, TILE)
    activated, grad_before, keep, give = call_on_vmem(
        middle_body,
        [jax.ShapeDtypeStruct(block, dtype) for dtype in (BF16, BF16, F32, F32)],
        *terms,
        arguments=(w_out, w_in, cotangent),
    )
    weights = SumEverywhere(keep, give)
    terms = propagate(grad_before, lists, [], weights)
    with jax.named_scope("weights"):
        grad_w_out, grad_w_in = weights.result()
    grad_features = call_on_vmem(
        end_body, jax.ShapeDtypeStruct(block, BF16), *terms, arguments=(w_out, w_in)
    )
    return activated, grad_features, grad_w_out, grad_w_in


def solution(mesh):
    placed = (
        P(("row", "col"), None),
        P(),
        P(),
        P("row", "col", None),
        P("row", "col"),
        P("row", "col", None, None, None),
        P(("row", "col"), None),
    )
    return jax.shard_map(
        local,
        mesh=mesh,
        in_specs=placed,
        out_specs=(P(("row", "col"), None), P(("row", "col"), None), P(), P()),
        check_vma=False,
    )
```

```python
import jax
import jax.numpy as jnp
from jax import lax
from jax.experimental import pallas as pl
from jax.experimental.pallas import tpu as pltpu
from jax.sharding import PartitionSpec as P

TILE = 256
LISTED = 16
F32 = jnp.float32
BF16 = jnp.bfloat16

ROWS = 32
COLS = 8


def moved(step):
    pairs = []
    for at in range(ROWS * COLS):
        r, c = at // COLS, at % COLS
        z, hi, core, lo, y = step(r // 4, r // 2 % 2, r % 2, c // 4, c % 4)
        pairs.append((at, (((z % 8) * 2 + hi) * 2 + core) * COLS + lo * 4 + y % 4))
    return pairs


def permute(x, step):
    return lax.ppermute(x, ("row", "col"), moved(step))


def swap_core(x):
    return permute(x, lambda z, hi, core, lo, y: (z, hi, 1 - core, lo, y))


def swap_hi(x):
    return permute(x, lambda z, hi, core, lo, y: (z, 1 - hi, core, lo, y))


def along_z(x):
    return permute(x, lambda z, hi, core, lo, y: (z + 1 - 2 * core, hi, core, lo, y))


def twice_along_z(x):
    return permute(x, lambda z, hi, core, lo, y: (z + 2 - 4 * core, hi, core, lo, y))


def along_z_to_hi(x):
    return permute(x, lambda z, hi, core, lo, y: (z + 1 - 2 * core, 1 - hi, core, lo, y))


def along_y_to_lo(x):
    return permute(x, lambda z, hi, core, lo, y: (z, hi, core, 1 - lo, y + 1 - 2 * core))


def across_y_to_lo(x):
    return permute(x, lambda z, hi, core, lo, y: (z, hi, core, 1 - lo, y + 2))


def along_y(x):
    return permute(x, lambda z, hi, core, lo, y: (z, hi, core, lo, y + 1 - 2 * core))


def across_y(x):
    return permute(x, lambda z, hi, core, lo, y: (z, hi, core, lo, y + 2))


def swap_lo(x):
    return permute(x, lambda z, hi, core, lo, y: (z, hi, core, 1 - lo, y))


def exchange_rows(x):
    return lax.all_to_all(x, "col", 0, 0, tiled=True)


def place():
    row, col = lax.axis_index("row"), lax.axis_index("col")
    return row >> 2, (row >> 1) & 1, row & 1, col >> 2, col & 3


def column_at(where, tile_col, forward):
    z, hi, core, _, _ = where
    dz = ((tile_col >> 2) - z) & 7
    j = jnp.where(core == (1 if forward else 0), dz, (8 - dz) & 7)
    k = (tile_col & 1) ^ core
    f = ((tile_col >> 1) & 1) ^ hi
    ends = jnp.logical_or(j == 0, j == 4)
    mine = jnp.logical_or(jnp.logical_and(j >= 1, j <= 3), jnp.logical_and(ends, k == 0))
    if forward:
        return mine, f + jnp.where(ends, 12 + (j >> 1), (j - 1) * 4 + k * 2)
    inner = jnp.where(j == 3, 9, (j - 1) * 4) + f * 2 + k
    return mine, jnp.where(j == 0, 8 + f * 7, jnp.where(j == 4, 13 + f, inner))


def sum_row_at(where, which, tile_row):
    _, _, core, lo, y = where
    f = (tile_row >> 2) ^ lo
    dy = ((tile_row & 3) - y) & 3
    along = dy == 1 + 2 * core
    near = f * 2 + jnp.where(along, which, 8 + 1 - which)
    return jnp.where(dy == 0, 6 + f + which * 8, jnp.where(dy == 2, 4 + f + which * 8, near))


ANYWHERE = pl.BlockSpec(memory_space=pl.ANY)
IN_HBM = pl.BlockSpec(memory_space=pltpu.HBM)
INTEGERS = pl.BlockSpec(memory_space=pltpu.SMEM)


def together(*arrays):
    return lax.optimization_barrier(arrays)


def tile_kernel(forward, sizes, *refs):
    slots, counts, tiles = refs[0:2], refs[2:4], refs[4:6]
    sources = refs[6 : 6 + len(sizes)]
    outs = refs[6 + len(sizes) : -3]
    total, side, todo = refs[-3:]
    where = place()

    counted = []
    for which in range(2):

        def note(k, n):
            slot = slots[which][0, 0, k]
            mine, col_at = column_at(where, slot & 31, forward)
            row_at = slot >> 5
            if forward:
                row_at = sum_row_at(where, which, slot >> 5)

            @pl.when(mine)
            def _():
                todo[which, 0, n] = k
                todo[which, 1, n] = col_at if forward else row_at
                todo[which, 2, n] = row_at if forward else col_at

            return n + mine.astype(jnp.int32)

        counted.append(lax.fori_loop(0, counts[which][0, 0], note, 0))

    total[...] = jnp.zeros_like(total)
    if forward:
        first = 0
        for source, n in zip(sources, sizes):
            side[first : first + n] = source[:n]
            first += n

    def product(which, tile, at):
        if forward:
            return jnp.dot(tile, side[at], preferred_element_type=F32)
        return lax.dot_general(
            tile,
            sources[which][at, :TILE],
            (((0,), (0,)), ((), ())),
            preferred_element_type=F32,
        )

    for which in range(2):
        n = counted[which]

        def step(p, carry):
            products = []
            for u in range(2):
                i = 2 * p + u
                real = i < n
                i = jnp.where(real, i, 2 * p)
                value = product(which, tiles[which][todo[which, 0, i]], todo[which, 1, i])
                products.append((jnp.where(real, todo[which, 2, i], 16), value))
            for at, value in products:
                total[at] += value
            return carry

        lax.fori_loop(0, (n + 1) >> 1, step, 0)
    first = 0
    for out in outs:
        out[...] = total[first : first + out.shape[0]].astype(out.dtype)
        first += out.shape[0]


def tile_call(forward, lists, sizes, sources):
    def kernel(*refs):
        tile_kernel(forward, sizes, *refs)

    vmem = pl.BlockSpec(memory_space=pltpu.VMEM)
    block = (TILE, TILE)
    kept, home, sent = (6, 2, (8,)) if forward else (8, 1, (4, 2, 1))
    return pl.pallas_call(
        kernel,
        out_shape=[jax.ShapeDtypeStruct((n,) + block, F32) for n in (kept, home)]
        + [jax.ShapeDtypeStruct((n,) + block, BF16) for n in sent],
        in_specs=[INTEGERS] * 4 + [vmem] * (2 + len(sources)),
        out_specs=[vmem] * (2 + len(sent)),
        scratch_shapes=[
            pltpu.VMEM((17,) + block, F32),
            pltpu.VMEM((16,) + block, BF16),
            pltpu.SMEM((2, 3, LISTED), jnp.int32),
        ],
        compiler_params=pltpu.CompilerParams(vmem_limit_bytes=24 * 2**20),
        cost_estimate=pl.CostEstimate(
            flops=16 * 2 * TILE**3,
            bytes_accessed=(100 if forward else 40) * 2**20,
            transcendentals=0,
        ),
    )(*lists, *sources)


def dot2(x, y, dims):
    high = x.astype(BF16)
    low = (x - high.astype(F32)).astype(BF16)
    return lax.dot_general(high, y, (dims, ((), ())), preferred_element_type=F32) + lax.dot_general(
        low, y, (dims, ((), ())), preferred_element_type=F32
    )


def fetch_all(pairs, sems):
    copies = [pltpu.make_async_copy(a, b, sems.at[i]) for i, (a, b) in enumerate(pairs)]
    for copy in copies:
        copy.start()
    for copy in copies:
        copy.wait()


def call_on_vmem(body, out_shape, *operands, arguments=()):
    operands = operands + tuple(arguments)
    arrays = [x[0] if isinstance(x, tuple) else x for x in operands]
    parts = [x[1] if isinstance(x, tuple) else None for x in operands]
    n, first_argument = len(arrays), len(arrays) - len(arguments)
    copied = []
    for i, (x, part) in enumerate(zip(arrays, parts)):
        if i >= first_argument or (part is not None and x.shape[0] > 2):
            copied.append(i)
    shapes = []
    for i in copied:
        x, part = arrays[i], parts[i]
        shape = x.shape if part is None else jax.eval_shape(lambda v, p=part: v[p], x).shape
        shapes.append(pltpu.VMEM(shape, x.dtype))

    def kernel(*refs):
        sources, outs = list(refs[:n]), refs[n : len(refs) - len(copied) - 1]
        held, sems = refs[len(refs) - len(copied) - 1 : -1], refs[-1]
        pairs = []
        for i, to in zip(copied, held):
            pairs.append((sources[i] if parts[i] is None else sources[i].at[parts[i]], to))
        fetch_all(pairs, sems)
        for i, to in zip(copied, held):
            sources[i] = to
        for i, part in enumerate(parts):
            if part is not None and i not in copied:
                sources[i] = sources[i].at[part]
        body(*sources, *outs)

    vmem = pl.BlockSpec(memory_space=pltpu.VMEM)
    specs = []
    for i in range(n):
        specs.append(IN_HBM if i >= first_argument else ANYWHERE if i in copied else vmem)
    return pl.pallas_call(
        kernel,
        out_shape=out_shape,
        in_specs=specs,
        out_specs=jax.tree.map(lambda _: vmem, out_shape),
        scratch_shapes=shapes + [pltpu.SemaphoreType.DMA((max(len(copied), 1),))],
        compiler_params=pltpu.CompilerParams(vmem_limit_bytes=16 * 2**20),
        cost_estimate=pl.CostEstimate(
            flops=8 * 2 * TILE**3, bytes_accessed=4 * 2**20, transcendentals=TILE * TILE
        ),
    )(*arrays)


N_ROW_TERMS, N_COL_TERMS = 9, 6


def sum_of(terms):
    total = terms[0][...].astype(F32)
    for term in terms[1:]:
        total = total + term[...].astype(F32)
    return total


def sums_of(terms):
    return sum_of(terms[:N_ROW_TERMS]), sum_of(terms[N_ROW_TERMS:])


def middle_body(*refs):
    out_sum, in_sum = sums_of(refs[: N_ROW_TERMS + N_COL_TERMS])
    w_out, w_in, cotangent, activated, grad_before, keep, give = refs[
        N_ROW_TERMS + N_COL_TERMS :
    ]
    before = dot2(out_sum, w_out[...], ((1,), (0,))) + dot2(in_sum, w_in[...], ((1,), (0,)))
    gate = jax.nn.sigmoid(before)
    activated[...] = (before * gate).astype(BF16)
    grad = (cotangent[...].astype(F32) * gate * (1.0 + before * (1.0 - gate))).astype(BF16)
    grad_before[...] = grad
    first = place()[2] == 0
    local_out = dot2(out_sum, grad, ((0,), (0,)))
    local_in = dot2(in_sum, grad, ((0,), (0,)))
    keep[...] = jnp.where(first, local_out, local_in)
    give[...] = jnp.where(first, local_in, local_out)


def end_body(*refs):
    back_forward, back_transposed = sums_of(refs[: N_ROW_TERMS + N_COL_TERMS])
    w_out, w_in, grad_features = refs[N_ROW_TERMS + N_COL_TERMS :]
    grad_features[...] = (
        dot2(back_transposed, w_out[...], ((1,), (1,)))
        + dot2(back_forward, w_in[...], ((1,), (1,)))
    ).astype(BF16)


def add(parts, *arrived):
    for x in arrived:
        parts = parts + x.astype(F32)
    return parts.astype(BF16)


class Nothing:
    def rows_out(self, source):
        def body(source, out):
            for i in range(COLS):
                out[i] = source[0]

        return call_on_vmem(body, jax.ShapeDtypeStruct((COLS, TILE, TILE), BF16), source)

    def rows_arrived(self, rows):
        pass

    def send(self):
        return ()

    def take(self, arrived):
        pass

    def join(self, *after):
        pass


def two_terms(x):
    high = x.astype(BF16)
    return high, (x - high.astype(F32)).astype(BF16)


PIECE = TILE // COLS


class SumEverywhere:
    def __init__(self, keep, give):
        self.keep, self.give = keep, give
        self.moves = [
            swap_hi,
            self.flip_z(1),
            self.flip_z(2),
            self.flip_z(4),
        ]

    def flip_z(self, bit):
        return lambda x: permute(x, lambda z, hi, core, lo, y: (z ^ bit, hi, core, lo, y))

    def rows_out(self, source):
        def body(source, keep, given, out):
            for i in range(COLS):
                at = slice(i * PIECE, (i + 1) * PIECE)
                out[i, :TILE] = source[0]
                high, low = two_terms(keep[at] + given[at])
                out[i, TILE : TILE + PIECE] = high
                out[i, TILE + PIECE :] = low

        shape = jax.ShapeDtypeStruct((COLS, TILE + 2 * PIECE, TILE), BF16)
        return call_on_vmem(body, shape, source, self.keep, swap_core(self.give))

    def rows_arrived(self, rows):
        def body(part, out):
            total = part[0].astype(F32)
            for i in range(1, COLS):
                total = total + part[i].astype(F32)
            out[...] = total[:PIECE] + total[PIECE:]

        shape = jax.ShapeDtypeStruct((PIECE, TILE), F32)
        self.total = call_on_vmem(body, shape, (rows, (slice(None), slice(TILE, None))))

    def send(self):
        with jax.named_scope("weights"):
            return (self.moves.pop(0)(self.total),)

    def take(self, arrived):
        with jax.named_scope("weights"):
            self.total = self.total + arrived[0]

    def join(self, *after):
        total, *_ = together(self.total, *after)
        self.mine = exchange_rows(jnp.broadcast_to(total, (COLS, PIECE, TILE)))

    def result(self):
        mine = self.mine.reshape(TILE, TILE)
        whole = jax.ShapeDtypeStruct((TILE, TILE), F32)
        return call_on_vmem(order_kernel, [whole] * 2, mine, swap_core(mine))


def order_kernel(mine, theirs, first, second):
    @pl.when(place()[2] == 0)
    def _():
        first[...] = mine[...]
        second[...] = theirs[...]

    @pl.when(place()[2] == 1)
    def _():
        first[...] = theirs[...]
        second[...] = mine[...]


def propagate(source, lists, early, beside):
    source = source[None]
    with jax.named_scope("gather"):
        from_hi = swap_hi(source)
        rows = beside.rows_out(source)
        rows, from_hi = together(rows, from_hi)
        rows = exchange_rows(rows)
        twin = swap_core(source)
        z0 = jnp.concatenate([source, from_hi, twin, swap_core(from_hi)])
        z1 = along_z(z0)
        z2 = along_z(z1)
        rows, z1, *_ = together(rows, z1, *early)
        beside.rows_arrived(rows)
        rows_twin, z2, *sent = together(swap_core(rows), z2, *beside.send())
        beside.take(sent)
        z3 = along_z(z2)
        z4 = twice_along_z(z2[:2])

    with jax.named_scope("transposed"):
        kept, home, three, four, home_hi = tile_call(False, lists, (8, 8), [rows, rows_twin])
        z3, z4, *sent = together(z3, z4, *beside.send())
        beside.take(sent)
        three = along_z(three)
        four = twice_along_z(four)

    with jax.named_scope("forward"):
        sources = [z1, z2, z3, z0, z4]
        sums, home_row, other = tile_call(True, lists, (4, 4, 4, 2, 2), sources)
        other = swap_core(other)
        sums, three, four, *sent = together(sums, three, four, *beside.send())
        beside.take(sent)
        three = kept[4:8] + three.astype(F32)
        two = jnp.concatenate(
            [
                three[:1] + four[:1].astype(F32),
                three[1:2],
                three[2:3] + four[1:].astype(F32),
                three[3:],
            ]
        )
        two = along_z(two.astype(BF16))
        home_hi = swap_hi(home_hi)
        near = along_y(add(sums[:2], other[:2]))
        near_lo = along_y_to_lo(add(sums[2:4], other[2:4]))
        across = across_y(add(sums[4:5], other[4:5]))
        across_lo = across_y_to_lo(add(sums[5:6], other[5:6]))
        home_lo = swap_lo(add(home_row[1:], other[7:]))

    with jax.named_scope("sums"):
        two, near, near_lo, home_hi, *sent = together(
            two, near, near_lo, home_hi, *beside.send()
        )
        beside.take(sent)
        one_hi, one = together(add(kept[2:4], two[2:]), add(kept[:2], two[:2]))
        one_hi = along_z_to_hi(one_hi)
        one = along_z(one)
        beside.join(near, near_lo)
    return [
        (home_row, 0),
        (other, 6),
        (near, 0),
        (swap_core(near[1:]), 0),
        (near_lo, 0),
        (swap_core(near_lo[1:]), 0),
        (across, 0),
        (across_lo, 0),
        (home_lo, 0),
        (home, 0),
        (one, 0),
        (swap_core(one[1:]), 0),
        (one_hi, 0),
        (swap_core(one_hi[1:]), 0),
        (home_hi, 0),
    ]


def local(features, w_out, w_in, tile_slot, tile_count, tile_values, cotangent):
    tiles = tile_values[0, 0]
    other = [swap_core(tile_slot), swap_core(tile_count), swap_core(tiles)]
    lists = [tile_slot, other[0], tile_count, other[1], tiles, other[2]]

    terms = propagate(features, lists, other[:2], Nothing())
    block = (TILE, TILE)
    activated, grad_before, keep, give = call_on_vmem(
        middle_body,
        [jax.ShapeDtypeStruct(block, dtype) for dtype in (BF16, BF16, F32, F32)],
        *terms,
        arguments=(w_out, w_in, cotangent),
    )
    weights = SumEverywhere(keep, give)
    terms = propagate(grad_before, lists, [], weights)
    with jax.named_scope("weights"):
        grad_w_out, grad_w_in = weights.result()
    grad_features = call_on_vmem(
        end_body, jax.ShapeDtypeStruct(block, BF16), *terms, arguments=(w_out, w_in)
    )
    return activated, grad_features, grad_w_out, grad_w_in


def solution(mesh):
    placed = (
        P(("row", "col"), None),
        P(),
        P(),
        P("row", "col", None),
        P("row", "col"),
        P("row", "col", None, None, None),
        P(("row", "col"), None),
    )
    return jax.shard_map(
        local,
        mesh=mesh,
        in_specs=placed,
        out_specs=(P(("row", "col"), None), P(("row", "col"), None), P(), P()),
        check_vma=False,
    )
```
